128 devices in a mesh: prow: 8 (over x, core), pcol: 16 (over y, z).
Axes of the slice: x: 4, y: 4, z: 4, core: 2. Of those that a mesh axis runs over, the one named last changes fastest.
Arguments:
- z_block: float32 [131072, 2048], P('prow', 'pcol'), may hold values from -6 to 6
- v_panels: bfloat16 [2, 131072, 512], P(None, 'prow', 'pcol'), may hold values from -0.015625 to 0.015625
- t_panels: float32 [2, 512, 512], replicated, as said below
Outputs:
- eigen_out: float32 [131072, 2048], P('prow', 'pcol')
The draws below stay inside these ranges and needn't reach their ends.
Inputs may be any that keep to these rules, and one draw needn't show every extreme that they name: Each panel of t_panels is upper triangular with a positive diagonal.
All inputs are finite; a program needn't handle non-finite values.
Results may differ from the reference program's by a relative error of at most 0.0045.
Values may be sent and summed in bfloat16 or wider, within the bound.
No kernel may reach another device: no remote copies, remote signals or barrier semaphores. Data moves between devices by JAX's collectives and lax.ppermute only.
A program may use at most 128 MiB of HBM per device.

```python
import math
import jax
import jax.numpy as jnp
from jax import lax

NB = 512
NROWS = 131072
NEV = 2048


def draw_t_panels(key, part):
    key = jax.random.fold_in(key, 7)
    first, second = jax.random.split(key, 2)
    upper = jax.random.normal(first, (2, NB, NB), jnp.float32)
    upper = jnp.triu(upper, 1)
    diagonal = jnp.exp(jax.random.uniform(second, (2, NB), jnp.float32, 0.0, math.log(4.0)))
    identity = jnp.eye(NB, dtype=jnp.float32)
    return (upper + diagonal[:, :, None] * identity[None, :, :]).astype(jnp.float32)


def shard_levels(own_key, extent, cuts, smallest, high):
    def one(axis_at, blocks):
        draws = jax.random.uniform(jax.random.fold_in(jax.random.fold_in(own_key, 6), axis_at), (blocks,), jnp.float32, smallest / len(cuts), high / len(cuts))
        return jnp.repeat(jnp.exp(draws), extent[axis_at] // blocks).reshape((-1,) + (1,) * (len(extent) - axis_at - 1))

    loudness = one(*cuts[0])
    for cut in cuts[1:]:
        loudness = loudness * one(*cut)
    return loudness


def scatter_about(stream_key, dims, scale, most, cuts=(), held_as=jnp.bfloat16):
    factor_of = shard_levels(stream_key, dims, cuts, -0.22, 0.18) if cuts else 1.0
    values = jax.random.normal(stream_key, dims, jnp.float32) * scale * factor_of
    return jnp.minimum(jnp.maximum(values, -most), most).astype(held_as)


def setup_inputs(seed: int = 0) -> dict:
    key_of = jax.random.split(jax.random.key(seed), 4)
    z_block = scatter_about(key_of[0], (NROWS, NEV), 1.0, 6.0, ((0, 8), (1, 16)), jnp.float32)
    v_panels = scatter_about(key_of[1], (2, NROWS, NB), NROWS ** -0.5, 0.015625, ((1, 8), (2, 16)))
    t_panels = draw_t_panels(jax.random.fold_in(key_of[3], 71), 0)
    return dict(z_block=z_block, v_panels=v_panels, t_panels=t_panels)


def reference(z_block, v_panels, t_panels):
    vectors = z_block
    for which_panel in range(2):
        reflectors = v_panels[which_panel]
        rounded = vectors.astype(jnp.bfloat16)
        partial_value = lax.dot_general(reflectors, rounded, (((0,), (0,)), ((), ())), preferred_element_type=jnp.float32)
        coeffs = jnp.dot(t_panels[which_panel].T, partial_value, precision=lax.Precision.HIGHEST).astype(jnp.bfloat16)
        vectors = vectors - jnp.dot(reflectors, coeffs, preferred_element_type=jnp.float32)
    return vectors
```

```python
import functools

import jax
import jax.numpy as jnp
from jax import lax
from jax.experimental import pallas as pl
from jax.experimental.pallas import tpu as pltpu
from jax.sharding import PartitionSpec as P

RING = 4
BF16, F32 = jnp.bfloat16, jnp.float32
AXES = ("prow", "pcol")


def device(x, core, y, z):
    return (x * 2 + core) * RING * RING + y * RING + z


def permutation(target):
    pairs = []
    for x in range(RING):
        for core in range(2):
            for y in range(RING):
                for z in range(RING):
                    pairs.append((device(x, core, y, z), device(*target(x, core, y, z))))
    return pairs


def along_u(s):
    return permutation(lambda x, c, y, z: (x, c, (y + s) % RING, z) if c == 0 else (x, c, y, (z + s) % RING))


def along_w(s):
    return permutation(lambda x, c, y, z: (x, c, y, (z + s) % RING) if c == 0 else (x, c, (y + s) % RING, z))


def along_x(s):
    return permutation(lambda x, c, y, z: ((x + s) % RING, c, y, z))


def other_core():
    return permutation(lambda x, c, y, z: (x, 1 - c, y, z))


def send(value, pairs):
    return lax.ppermute(value, AXES, pairs)


def params(mib=48):
    return pltpu.CompilerParams(vmem_limit_bytes=mib * 2**20)


def cost(flops, nbytes):
    return pl.CostEstimate(flops=flops, bytes_accessed=nbytes, transcendentals=0)


def stack_kernel(place, *refs):
    out = refs[-1]
    width = refs[0].shape[0]
    for s in range(RING):
        at = lax.rem(place[0] - s + RING, RING)
        out[pl.ds(pl.multiple_of(at * width, width), width), :] = refs[s][...]


def stack(place, blocks):
    width, rows = blocks[0].shape
    tile = rows // 4
    return pl.pallas_call(
        stack_kernel,
        grid_spec=pltpu.PrefetchScalarGridSpec(
            num_scalar_prefetch=1,
            grid=(rows // tile,),
            in_specs=[pl.BlockSpec((width, tile), lambda i, place: (0, i))] * RING,
            out_specs=pl.BlockSpec((RING * width, tile), lambda i, place: (0, i)),
        ),
        out_shape=jax.ShapeDtypeStruct((RING * width, rows), BF16),
        compiler_params=params(),
        cost_estimate=cost(0, 4 * RING * width * rows),
        name="stack_reflectors",
    )(place, *blocks)


def transpose_kernel(*refs):
    out = refs[-1]
    width = refs[0].shape[0]
    for t in range(RING):
        out[:, t * width:(t + 1) * width] = refs[t][...].T


def transpose(blocks):
    width, rows = blocks[0].shape
    tile = 512
    return pl.pallas_call(
        transpose_kernel,
        grid=(rows // tile,),
        in_specs=[pl.BlockSpec((width, tile), lambda i: (0, i))] * RING,
        out_specs=pl.BlockSpec((tile, RING * width), lambda i: (i, 0)),
        out_shape=jax.ShapeDtypeStruct((rows, RING * width), BF16),
        compiler_params=params(),
        cost_estimate=cost(0, 4 * RING * width * rows),
        name="transpose_reflectors",
    )(*blocks)


def first_sums_kernel(*refs):
    v, z, outs, total = refs[:4], refs[4:8], refs[8:12], refs[12]
    step = pl.program_id(0)

    @pl.when(step == 0)
    def _():
        total[...] = jnp.zeros_like(total)

    left = jnp.concatenate([r[...] for r in v], axis=0)
    right = jnp.concatenate([r[...] for r in z], axis=1)
    total[...] += jnp.dot(left, right, preferred_element_type=F32)

    @pl.when(step == pl.num_programs(0) - 1)
    def _():
        for s in range(RING):
            outs[s][...] = total[:, s * 128:(s + 1) * 128].astype(outs[s].dtype)


def second_sums_kernel(*refs):
    v, z, flat, coeffs, outs, total = refs[:4], refs[4:8], refs[8], refs[9:13], refs[13:17], refs[17]
    step = pl.program_id(0)

    @pl.when(step == 0)
    def _():
        total[...] = jnp.zeros_like(total)

    left = jnp.concatenate([r[...] for r in v], axis=0)
    old = jnp.concatenate([r[...] for r in z], axis=1).astype(F32)
    w = jnp.concatenate([r[...] for r in coeffs], axis=1)
    right = (old - jnp.dot(flat[...], w, preferred_element_type=F32)).astype(BF16)
    total[...] += jnp.dot(left, right, preferred_element_type=F32)

    @pl.when(step == pl.num_programs(0) - 1)
    def _():
        for s in range(RING):
            outs[s][...] = total[:, s * 128:(s + 1) * 128].astype(outs[s].dtype)


def sums(v, z, flat=None, coeffs=None):
    width, rows = v[0].shape
    columns = z[0].shape[1]
    nb = RING * width
    tile = 512
    in_specs = [pl.BlockSpec((width, tile), lambda i: (0, i))] * RING
    in_specs += [pl.BlockSpec((tile, columns), lambda i: (i, 0))] * RING
    args = list(v) + list(z)
    if flat is not None:
        in_specs += [pl.BlockSpec((tile, nb), lambda i: (i, 0))]
        in_specs += [pl.BlockSpec((nb, columns), lambda i: (0, 0))] * RING
        args += [flat] + list(coeffs)
    return pl.pallas_call(
        first_sums_kernel if flat is None else second_sums_kernel,
        grid=(rows // tile,),
        in_specs=in_specs,
        out_specs=[pl.BlockSpec((nb, columns), lambda i: (0, 0))] * RING,
        out_shape=[jax.ShapeDtypeStruct((nb, columns), F32 if s == 0 else BF16) for s in range(RING)],
        scratch_shapes=[pltpu.VMEM((nb, RING * columns), F32)],
        compiler_params=params(),
        cost_estimate=cost(2 * nb * rows * RING * columns * (1 if flat is None else 2), 4 * nb * rows),
        name="panel_sums",
    )(*args)


def add_cores_kernel(place, mine, theirs, out):
    u, w = place[0], place[1]
    width = mine.shape[0] // (RING * RING)
    for t in range(RING):
        for k in range(RING):
            at = lax.rem(u - k + RING, RING) * RING + lax.rem(w - t + RING, RING)
            rows = slice((t * RING + k) * width, (t * RING + k + 1) * width)
            out[rows, :] = mine[rows, :] + theirs[pl.ds(pl.multiple_of(at * width, width), width), :]


def add_cores(place, mine, theirs):
    vmem = pl.BlockSpec(memory_space=pltpu.VMEM)
    return pl.pallas_call(
        add_cores_kernel,
        in_specs=[pl.BlockSpec(memory_space=pltpu.SMEM), vmem, vmem],
        out_specs=vmem,
        out_shape=jax.ShapeDtypeStruct(mine.shape, F32),
        compiler_params=params(),
        cost_estimate=cost(mine.size, 12 * mine.size),
        name="add_cores",
    )(place, mine, theirs)


def coefficients_kernel(factor, a, b, c, d, out):
    total = a[...] + b[...].astype(F32) + c[...].astype(F32) + d[...].astype(F32)
    out[...] = jnp.dot(
        factor[...], total, preferred_element_type=F32, precision=lax.Precision.HIGHEST
    ).astype(BF16)


def coefficients(factor, parts):
    vmem = pl.BlockSpec(memory_space=pltpu.VMEM)
    return pl.pallas_call(
        coefficients_kernel,
        in_specs=[vmem] * 5,
        out_specs=vmem,
        out_shape=jax.ShapeDtypeStruct(parts[0].shape, BF16),
        compiler_params=params(),
        cost_estimate=cost(12 * factor.size * parts[0].shape[1], 4 * factor.size),
        name="coefficients",
    )(factor, *parts)


def update_kernel(*refs):
    first, second, w0, w1, outs = refs[0], refs[1], refs[2:6], refs[6:10], refs[10:14]
    w0 = jnp.concatenate([r[...] for r in w0], axis=1)
    w1 = jnp.concatenate([r[...] for r in w1], axis=1)
    moved = jnp.dot(first[...], w0, preferred_element_type=F32)
    moved += jnp.dot(second[...], w1, preferred_element_type=F32)
    for s in range(RING):
        outs[s][...] = moved[:, s * 128:(s + 1) * 128].astype(BF16)


def update(first, second, w0, w1):
    rows, nb = first.shape
    columns = w0[0].shape[1]
    tile = 512
    flat = pl.BlockSpec((tile, nb), lambda i: (i, 0))
    small = pl.BlockSpec((nb, columns), lambda i: (0, 0))
    return pl.pallas_call(
        update_kernel,
        grid=(rows // tile,),
        in_specs=[flat, flat] + [small] * (2 * RING),
        out_specs=[pl.BlockSpec((tile, columns), lambda i: (i, 0))] * RING,
        out_shape=[jax.ShapeDtypeStruct((rows, columns), BF16)] * RING,
        compiler_params=params(),
        cost_estimate=cost(4 * nb * rows * RING * columns, 4 * nb * rows),
        name="update",
    )(first, second, *w0, *w1)


def subtract_kernel(place, z, *refs):
    out = refs[-1]
    for s in range(RING):
        @pl.when(pl.program_id(0) == s)
        def _(s=s):
            out[...] = z[...] - refs[s][...].astype(F32)


def subtract(place, z, moved):
    rows, columns = moved[0].shape
    tile = 2048
    steps = rows // tile

    def whole(s, i, place):
        return (lax.rem(place[0] + s, RING) * steps + i, 0)

    def part(k):
        return lambda s, i, place: (jnp.where(s < k, 0, jnp.where(s == k, i, steps - 1)), 0)

    return pl.pallas_call(
        subtract_kernel,
        grid_spec=pltpu.PrefetchScalarGridSpec(
            num_scalar_prefetch=1,
            grid=(RING, steps),
            in_specs=[pl.BlockSpec((tile, columns), whole)]
            + [pl.BlockSpec((tile, columns), part(k)) for k in range(RING)],
            out_specs=pl.BlockSpec((tile, columns), whole),
        ),
        out_shape=jax.ShapeDtypeStruct(z.shape, F32),
        compiler_params=params(),
        cost_estimate=cost(z.size, 10 * z.size),
        name="subtract",
    )(place, z, *moved)


def rows_kernel(order, source, out):
    out[...] = source[...]


def take_blocks(order, source):
    nb = source.shape[1]
    width = nb // (RING * RING)
    return pl.pallas_call(
        rows_kernel,
        grid_spec=pltpu.PrefetchScalarGridSpec(
            num_scalar_prefetch=1,
            grid=(RING * RING,),
            in_specs=[pl.BlockSpec((2, width, nb), lambda i, order: (0, order[i], 0))],
            out_specs=pl.BlockSpec((2, width, nb), lambda i, order: (0, i, 0)),
        ),
        out_shape=jax.ShapeDtypeStruct(source.shape, F32),
        compiler_params=params(),
        cost_estimate=cost(0, 8 * source.size),
        name="take_blocks",
    )(order, source)


def local(z_block, v_panels, t_panels):
    prow, pcol = lax.axis_index("prow"), lax.axis_index("pcol")
    core, y, z = prow % 2, pcol // RING, pcol % RING
    u, w = jnp.where(core == 0, y, z), jnp.where(core == 0, z, y)
    place = jnp.stack([u, w]).astype(jnp.int32)
    rows = z_block.shape[0] // RING
    width = v_panels.shape[2]

    def chunk(s):
        return ((u + s) % RING) * rows

    def gather(panel):
        flat = v_panels[panel].T
        mine = [lax.dynamic_slice(flat, (0, chunk(s)), (width, rows)) for s in range(RING)]
        mine = [mine[0]] + [send(mine[s], along_u(s)) for s in range(1, RING)]
        block = stack(place, mine)
        return [block] + [send(block, along_w(t)) for t in range(1, RING)]

    step, kept = jnp.arange(RING * RING) // RING, jnp.arange(RING * RING) % RING
    gone = (w - step) % RING
    order = jnp.where(core == 0, kept * RING + gone, gone * RING + kept).astype(jnp.int32)
    factors = take_blocks(order, jnp.swapaxes(take_blocks(order, t_panels), 1, 2))

    def reduce(parts, factor):
        parts = [parts[0]] + [send(parts[s], along_u(-s)) for s in range(1, RING)]
        total = parts[0]
        for part in parts[1:]:
            total = total + part.astype(F32)
        total = add_cores(place, total, send(total, other_core()))
        rounded = total.astype(BF16)
        coeffs = coefficients(factor, [total] + [send(rounded, along_x(s)) for s in range(1, RING)])
        return [coeffs] + [send(coeffs, along_u(s)) for s in range(1, RING)]

    first = gather(0)
    dealt = [lax.dynamic_slice(z_block, (chunk(s), 0), (rows, z_block.shape[1])).astype(BF16) for s in range(RING)]
    dealt = [dealt[0]] + [send(dealt[s], along_u(s)) for s in range(1, RING)]
    second = gather(1)
    first_flat, second_flat = transpose(first), transpose(second)

    w0 = reduce(sums(first, dealt), factors[0])
    w1 = reduce(sums(second, dealt, first_flat, w0), factors[1])
    moved = update(first_flat, second_flat, w0, w1)
    moved = [moved[0]] + [send(moved[s], along_u(-s)) for s in range(1, RING)]
    return subtract(place, z_block, moved)


def solution(mesh):
    return jax.shard_map(
        local,
        mesh=mesh,
        in_specs=(P("prow", "pcol"), P(None, "prow", "pcol"), P()),
        out_specs=P("prow", "pcol"),
        check_vma=False,
    )
```

```python
import functools

import jax
import jax.numpy as jnp
from jax import lax
from jax.experimental import pallas as pl
from jax.experimental.pallas import tpu as pltpu
from jax.sharding import PartitionSpec as P

RING = 4
BF16, F32 = jnp.bfloat16, jnp.float32
AXES = ("prow", "pcol")


def device(x, core, y, z):
    return (x * 2 + core) * RING * RING + y * RING + z


def permutation(target):
    pairs = []
    for x in range(RING):
        for core in range(2):
            for y in range(RING):
                for z in range(RING):
                    pairs.append((device(x, core, y, z), device(*target(x, core, y, z))))
    return pairs


def along_u(s):
    return permutation(lambda x, c, y, z: (x, c, (y + s) % RING, z) if c == 0 else (x, c, y, (z + s) % RING))


def along_w(s):
    return permutation(lambda x, c, y, z: (x, c, y, (z + s) % RING) if c == 0 else (x, c, (y + s) % RING, z))


def along_x(s):
    return permutation(lambda x, c, y, z: ((x + s) % RING, c, y, z))


def other_core():
    return permutation(lambda x, c, y, z: (x, 1 - c, y, z))


def send(value, pairs):
    return lax.ppermute(value, AXES, pairs)


def params(mib=16):
    return pltpu.CompilerParams(vmem_limit_bytes=mib * 2**20)


def cost(flops, nbytes):
    return pl.CostEstimate(flops=flops, bytes_accessed=nbytes, transcendentals=0)


def home(place, t, k):
    gone = lax.rem(place[1] - t + RING, RING)
    return jnp.where(place[2] == 0, k * RING + gone, gone * RING + k)


def block_rows(at, width):
    return pl.ds(pl.multiple_of(at * width, width), width)


def stack_kernel(place, *refs):
    blocks, outs = refs[:RING], refs[RING:]
    width = blocks[0].shape[0] // 2
    for s in range(RING):
        rows = block_rows(lax.rem(place[0] - s + RING, RING), width)
        for panel in range(2):
            outs[panel][rows, :] = blocks[s][panel * width:(panel + 1) * width, :]


def stack(place, blocks):
    height, rows = blocks[0].shape
    tile = rows // 4
    out = jax.ShapeDtypeStruct((RING * height // 2, rows), BF16)
    return pl.pallas_call(
        stack_kernel,
        grid_spec=pltpu.PrefetchScalarGridSpec(
            num_scalar_prefetch=1,
            grid=(rows // tile,),
            in_specs=[pl.BlockSpec((height, tile), lambda i, place: (0, i))] * RING,
            out_specs=[pl.BlockSpec((RING * height // 2, tile), lambda i, place: (0, i))] * 2,
        ),
        out_shape=[out, out],
        compiler_params=params(8),
        cost_estimate=cost(0, 4 * RING * height * rows),
        name="stack_reflectors",
    )(place, *blocks)


def transpose_kernel(*refs):
    out = refs[-1]
    at = 0
    for r in refs[:-1]:
        out[:, at:at + r.shape[0]] = r[...].T
        at += r.shape[0]


def transpose(blocks):
    rows = blocks[0].shape[1]
    nb = sum(b.shape[0] for b in blocks)
    tile = 1024
    return pl.pallas_call(
        transpose_kernel,
        grid=(rows // tile,),
        in_specs=[pl.BlockSpec((b.shape[0], tile), lambda i: (0, i)) for b in blocks],
        out_specs=pl.BlockSpec((tile, nb), lambda i: (i, 0)),
        out_shape=jax.ShapeDtypeStruct((rows, nb), BF16),
        compiler_params=params(8),
        cost_estimate=cost(0, 4 * nb * rows),
        name="transpose_reflectors",
    )(*blocks)


def put_home(place, total, outs, width):
    for s in range(RING):
        for t in range(RING):
            for k in range(RING):
                at = t * RING + k
                outs[s][block_rows(home(place, t, k), width), :] = total[
                    at * width:(at + 1) * width, s * 128:(s + 1) * 128
                ].astype(outs[s].dtype)


def take_home(place, sources, width, out):
    for s, source in enumerate(sources):
        for t in range(RING):
            for k in range(RING):
                at = t * RING + k
                out[at * width:(at + 1) * width, s * 128:(s + 1) * 128] = source[block_rows(home(place, t, k), width), :]


def first_sums_kernel(count, width, place, *refs):
    v, z = refs[:count], refs[count:count + RING]
    outs, total = refs[count + RING:count + 2 * RING], refs[-1]
    step = pl.program_id(0)
    left = jnp.concatenate([r[...] for r in v], axis=0)
    right = jnp.concatenate([r[...] for r in z], axis=1)
    part = jnp.dot(left, right, preferred_element_type=F32)

    @pl.when(step == 0)
    def _():
        total[...] = part

    @pl.when(step > 0)
    def _():
        total[...] += part

    @pl.when(step == pl.num_programs(0) - 1)
    def _():
        put_home(place, total, outs, width)


def second_sums_kernel(count, width, place, *refs):
    v, z, flat = refs[:count], refs[count:count + RING], refs[count + RING]
    coeffs, outs = refs[count + RING + 1:count + 2 * RING + 1], refs[count + 2 * RING + 1:count + 3 * RING + 1]
    total, w = refs[-2:]
    step = pl.program_id(0)

    @pl.when(step == 0)
    def _():
        take_home(place, coeffs, width, w)

    left = jnp.concatenate([r[...] for r in v], axis=0)
    old = jnp.concatenate([r[...] for r in z], axis=1).astype(F32)
    right = (old - jnp.dot(flat[...], w[...], preferred_element_type=F32)).astype(BF16)
    part = jnp.dot(left, right, preferred_element_type=F32)

    @pl.when(step == 0)
    def _():
        total[...] = part

    @pl.when(step > 0)
    def _():
        total[...] += part

    @pl.when(step == pl.num_programs(0) - 1)
    def _():
        put_home(place, total, outs, width)


SUMS_TILE = 1024


def sums(place, v, z, flat=None, coeffs=None, tile=None):
    tile = tile or SUMS_TILE
    rows = v[0].shape[1]
    columns = z[0].shape[1]
    nb = sum(b.shape[0] for b in v)
    width = nb // (RING * RING)
    in_specs = [pl.BlockSpec((b.shape[0], tile), lambda i, place: (0, i)) for b in v]
    in_specs += [pl.BlockSpec((tile, columns), lambda i, place: (i, 0))] * RING
    args = list(v) + list(z)
    scratch = [pltpu.VMEM((nb, RING * columns), F32)]
    if flat is not None:
        in_specs += [pl.BlockSpec((tile, nb), lambda i, place: (i, 0))]
        in_specs += [pl.BlockSpec((nb, columns), lambda i, place: (0, 0))] * RING
        args += [flat] + list(coeffs)
        scratch += [pltpu.VMEM((nb, RING * columns), BF16)]
    return pl.pallas_call(
        functools.partial(first_sums_kernel if flat is None else second_sums_kernel, len(v), width),
        grid_spec=pltpu.PrefetchScalarGridSpec(
            num_scalar_prefetch=1,
            grid=(rows // tile,),
            in_specs=in_specs,
            out_specs=[pl.BlockSpec((nb, columns), lambda i, place: (0, 0))] * RING,
            scratch_shapes=scratch,
        ),
        out_shape=[jax.ShapeDtypeStruct((nb, columns), F32 if s == 0 else BF16) for s in range(RING)],
        compiler_params=params(20),
        cost_estimate=cost(2 * nb * rows * RING * columns * (1 if flat is None else 2), 4 * nb * rows),
        name="panel_sums",
    )(place, *args)


def coefficients_kernel(factor, a, b, c, d, out):
    total = a[...] + b[...].astype(F32) + c[...].astype(F32) + d[...].astype(F32)
    out[...] = jnp.dot(
        factor[...], total, preferred_element_type=F32, precision=lax.Precision.HIGHEST
    ).astype(BF16)


def coefficients(factor, parts):
    vmem = pl.BlockSpec(memory_space=pltpu.VMEM)
    return pl.pallas_call(
        coefficients_kernel,
        in_specs=[vmem] * 5,
        out_specs=vmem,
        out_shape=jax.ShapeDtypeStruct(parts[0].shape, BF16),
        compiler_params=params(8),
        cost_estimate=cost(12 * factor.size * parts[0].shape[1], 4 * factor.size),
        name="coefficients",
    )(factor, *parts)


def update_kernel(count, width, place, first, second, *refs):
    w0, w1, outs, w = refs[:count], refs[count:2 * count], refs[2 * count:3 * count], refs[-1]
    nb = first.shape[1]

    @pl.when(pl.program_id(0) == 0)
    def _():
        take_home(place, w0, width, w.at[:nb])
        take_home(place, w1, width, w.at[nb:])

    moved = jnp.dot(first[...], w[:nb, :], preferred_element_type=F32)
    moved += jnp.dot(second[...], w[nb:, :], preferred_element_type=F32)
    for s in range(count):
        outs[s][...] = moved[:, s * 128:(s + 1) * 128].astype(BF16)


UPDATE_TILE = 1024


def update(place, first, second, w0, w1, tile=None):
    tile = tile or UPDATE_TILE
    rows, nb = first.shape
    columns = w0[0].shape[1]
    count = len(w0)
    flat = pl.BlockSpec((tile, nb), lambda i, place: (i, 0))
    small = pl.BlockSpec((nb, columns), lambda i, place: (0, 0))
    return pl.pallas_call(
        functools.partial(update_kernel, count, nb // (RING * RING)),
        grid_spec=pltpu.PrefetchScalarGridSpec(
            num_scalar_prefetch=1,
            grid=(rows // tile,),
            in_specs=[flat, flat] + [small] * (2 * count),
            out_specs=[pl.BlockSpec((tile, columns), lambda i, place: (i, 0))] * count,
            scratch_shapes=[pltpu.VMEM((2 * nb, count * columns), BF16)],
        ),
        out_shape=[jax.ShapeDtypeStruct((rows, columns), BF16)] * count,
        compiler_params=params(),
        cost_estimate=cost(4 * nb * rows * count * columns, 4 * nb * rows),
        name="update",
    )(place, first, second, *w0, *w1)


def subtract_kernel(s, place, z, moved, *refs):
    refs[-1][...] = z[...] - moved[...].astype(F32)


SUB_TILE = 2048


def subtract(place, z, moved, s, out, tile=None):
    tile = tile or SUB_TILE
    rows, columns = moved.shape
    steps = rows // tile

    def whole(i, place):
        return (lax.rem(place[0] + s, RING) * steps + i, 0)

    in_specs = [pl.BlockSpec((tile, columns), whole), pl.BlockSpec((tile, columns), lambda i, place: (i, 0))]
    args = [z, moved]
    if out is not None:
        in_specs.append(pl.BlockSpec(memory_space=pl.ANY))
        args.append(out)
    return pl.pallas_call(
        functools.partial(subtract_kernel, s),
        grid_spec=pltpu.PrefetchScalarGridSpec(
            num_scalar_prefetch=1,
            grid=(steps,),
            in_specs=in_specs,
            out_specs=pl.BlockSpec((tile, columns), whole),
        ),
        out_shape=jax.ShapeDtypeStruct(z.shape, F32),
        input_output_aliases={} if out is None else {3: 0},
        compiler_params=params(8),
        cost_estimate=cost(rows * columns, 10 * rows * columns),
        name="subtract",
    )(place, *args)


def local(z_block, v_panels, t_panels):
    prow, pcol = lax.axis_index("prow"), lax.axis_index("pcol")
    core, y, z = prow % 2, pcol // RING, pcol % RING
    u, w = jnp.where(core == 0, y, z), jnp.where(core == 0, z, y)
    place = jnp.stack([u, w, core]).astype(jnp.int32)
    rows = z_block.shape[0] // RING
    width = v_panels.shape[2]
    factors = jnp.swapaxes(t_panels, 1, 2)

    def chunk(s):
        return ((u + s) % RING) * rows

    def gather(block):
        half = block.shape[0] // 2
        ahead, behind = send(block, along_w(1)), send(block, along_w(-1))
        far_low = send(ahead[:half], along_w(1))
        far_high = send(behind[half:], along_w(-1))
        return [block, ahead, far_low, far_high, behind]

    flat = jnp.swapaxes(v_panels, 1, 2).reshape(2 * width, RING * rows)
    mine = [lax.dynamic_slice(flat, (0, chunk(s)), (2 * width, rows)) for s in range(RING)]
    z_in, mine = lax.optimization_barrier((z_block, mine))
    blocks = stack(place, [mine[0]] + [send(mine[s], along_u(s)) for s in range(1, RING)])

    dealt = [lax.dynamic_slice(z_in, (chunk(s), 0), (rows, z_block.shape[1])).astype(BF16) for s in range(RING)]
    dealt = [dealt[0]] + [send(dealt[s], along_u(s)) for s in range(1, RING)]
    first = gather(blocks[0])
    first, dealt, block, factors = lax.optimization_barrier((first, dealt, blocks[1], factors))
    near = [send(block, along_w(1)), send(block, along_w(-1))]

    def reduce(parts, factor, early, late):
        parts = [parts[0]] + [send(parts[s], along_u(-s)) for s in range(1, RING)]
        total = parts[0]
        for part in parts[1:]:
            total = total + part.astype(F32)
        total = total + send(total, other_core())
        rounded = total.astype(BF16)
        rounded, early = lax.optimization_barrier((rounded, early))
        parts = [total] + [send(rounded, along_x(s)) for s in range(1, RING)]
        parts, late = lax.optimization_barrier((parts, late))
        coeffs = coefficients(factor, parts)
        return [coeffs] + [send(coeffs, along_u(s)) for s in range(1, RING)], early, late

    w0, near, first_flat = reduce(sums(place, first, dealt), factors[0], near, transpose(first))
    second = [block, near[0], send(block, along_w(2)), near[1]]
    w1, _, second_flat = reduce(sums(place, second, dealt, first_flat, w0), factors[1], (), transpose(second))

    def moved(shifts):
        parts = update(place, first_flat, second_flat, [w0[s] for s in shifts], [w1[s] for s in shifts])
        return [part if s == 0 else send(part, along_u(-s)) for s, part in zip(shifts, parts)]

    right, left = moved((1, 3))
    far, own = moved((2, 0))
    out = subtract(place, z_block, own, 0, None)
    out = subtract(place, z_block, right, 1, out)
    out = subtract(place, z_block, left, 3, out)
    return subtract(place, z_block, far, 2, out)


def solution(mesh):
    return jax.shard_map(
        local,
        mesh=mesh,
        in_specs=(P("prow", "pcol"), P(None, "prow", "pcol"), P()),
        out_specs=P("prow", "pcol"),
        check_vma=False,
    )
```

```python
import functools

import jax
import jax.numpy as jnp
from jax import lax
from jax.experimental import pallas as pl
from jax.experimental.pallas import tpu as pltpu
from jax.sharding import PartitionSpec as P

RING = 4
BF16, F32 = jnp.bfloat16, jnp.float32
AXES = ("prow", "pcol")


def device(x, core, y, z):
    return (x * 2 + core) * RING * RING + y * RING + z


def permutation(target):
    pairs = []
    for x in range(RING):
        for core in range(2):
            for y in range(RING):
                for z in range(RING):
                    pairs.append((device(x, core, y, z), device(*target(x, core, y, z))))
    return pairs


def along_u(s):
    return permutation(lambda x, c, y, z: (x, c, (y + s) % RING, z) if c == 0 else (x, c, y, (z + s) % RING))


def along_w(s):
    return permutation(lambda x, c, y, z: (x, c, y, (z + s) % RING) if c == 0 else (x, c, (y + s) % RING, z))


def along_x(s):
    return permutation(lambda x, c, y, z: ((x + s) % RING, c, y, z))


def other_core():
    return permutation(lambda x, c, y, z: (x, 1 - c, y, z))


def send(value, pairs):
    return lax.ppermute(value, AXES, pairs)


def params(mib=16):
    return pltpu.CompilerParams(vmem_limit_bytes=mib * 2**20)


def cost(flops, nbytes):
    return pl.CostEstimate(flops=flops, bytes_accessed=nbytes, transcendentals=0)


def home(place, t, k):
    gone = lax.rem(place[1] - t + RING, RING)
    return jnp.where(place[2] == 0, k * RING + gone, gone * RING + k)


def block_rows(at, width):
    return pl.ds(pl.multiple_of(at * width, width), width)


def stack_kernel(place, *refs):
    blocks, outs = refs[:RING], refs[RING:]
    width = blocks[0].shape[0] // 2
    for s in range(RING):
        rows = block_rows(lax.rem(place[0] - s + RING, RING), width)
        for panel in range(2):
            outs[panel][rows, :] = blocks[s][panel * width:(panel + 1) * width, :]


def stack(place, blocks):
    height, rows = blocks[0].shape
    tile = rows // 4
    out = jax.ShapeDtypeStruct((RING * height // 2, rows), BF16)
    return pl.pallas_call(
        stack_kernel,
        grid_spec=pltpu.PrefetchScalarGridSpec(
            num_scalar_prefetch=1,
            grid=(rows // tile,),
            in_specs=[pl.BlockSpec((height, tile), lambda i, place: (0, i))] * RING,
            out_specs=[pl.BlockSpec((RING * height // 2, tile), lambda i, place: (0, i))] * 2,
        ),
        out_shape=[out, out],
        compiler_params=params(8),
        cost_estimate=cost(0, 4 * RING * height * rows),
        name="stack_reflectors",
    )(place, *blocks)


def transpose_kernel(*refs):
    out = refs[-1]
    at = 0
    for r in refs[:-1]:
        out[:, at:at + r.shape[0]] = r[...].T
        at += r.shape[0]


def transpose(blocks):
    rows = blocks[0].shape[1]
    nb = sum(b.shape[0] for b in blocks)
    tile = 1024
    return pl.pallas_call(
        transpose_kernel,
        grid=(rows // tile,),
        in_specs=[pl.BlockSpec((b.shape[0], tile), lambda i: (0, i)) for b in blocks],
        out_specs=pl.BlockSpec((tile, nb), lambda i: (i, 0)),
        out_shape=jax.ShapeDtypeStruct((rows, nb), BF16),
        compiler_params=params(8),
        cost_estimate=cost(0, 4 * nb * rows),
        name="transpose_reflectors",
    )(*blocks)


def put_home(place, total, outs, width):
    for s in range(RING):
        for t in range(RING):
            for k in range(RING):
                at = t * RING + k
                outs[s][block_rows(home(place, t, k), width), :] = total[
                    at * width:(at + 1) * width, s * 128:(s + 1) * 128
                ].astype(outs[s].dtype)


def take_home(place, sources, width, out):
    for s, source in enumerate(sources):
        for t in range(RING):
            for k in range(RING):
                at = t * RING + k
                out[at * width:(at + 1) * width, s * 128:(s + 1) * 128] = source[block_rows(home(place, t, k), width), :]


TILE = 1024


def tiles_of(z, tile):
    own, right, far_low, far_high, left = z
    steps = own.shape[0] // tile
    for i in range(steps):
        far = far_low if i < steps // 2 else far_high
        at = (i % (steps // 2)) * tile
        rows = slice(i * tile, (i + 1) * tile)
        yield rows, [own[rows, :], right[rows, :], far[at:at + tile, :], left[rows, :]]


def first_sums_kernel(count, width, place, *refs):
    v, z = refs[:count], refs[count:count + RING + 1]
    outs, total = refs[count + RING + 1:-1], refs[-1]
    for rows, parts in tiles_of(z, TILE):
        left = jnp.concatenate([r[:, rows] for r in v], axis=0)
        part = jnp.dot(left, jnp.concatenate(parts, axis=1), preferred_element_type=F32)
        if rows.start:
            total[...] += part
        else:
            total[...] = part
    put_home(place, total, outs, width)


def second_sums_kernel(count, width, place, *refs):
    v, z, flat = refs[:count], refs[count:count + RING + 1], refs[count + RING + 1]
    coeffs = refs[count + RING + 2:count + 2 * RING + 2]
    outs, total, w = refs[count + 2 * RING + 2:-2], refs[-2], refs[-1]
    take_home(place, coeffs, width, w)
    for rows, parts in tiles_of(z, TILE):
        left = jnp.concatenate([r[:, rows] for r in v], axis=0)
        old = jnp.concatenate(parts, axis=1).astype(F32)
        right = (old - jnp.dot(flat[rows, :], w[...], preferred_element_type=F32)).astype(BF16)
        part = jnp.dot(left, right, preferred_element_type=F32)
        if rows.start:
            total[...] += part
        else:
            total[...] = part
    put_home(place, total, outs, width)


def sums(place, v, z, flat=None, coeffs=()):
    vmem = pl.BlockSpec(memory_space=pltpu.VMEM)
    rows = v[0].shape[1]
    columns = z[0].shape[1]
    nb = sum(b.shape[0] for b in v)
    width = nb // (RING * RING)
    args = list(v) + list(z)
    scratch = [pltpu.VMEM((nb, RING * columns), F32)]
    if flat is not None:
        args += [flat, *coeffs]
        scratch += [pltpu.VMEM((nb, RING * columns), BF16)]
    return pl.pallas_call(
        functools.partial(first_sums_kernel if flat is None else second_sums_kernel, len(v), width),
        in_specs=[pl.BlockSpec(memory_space=pltpu.SMEM)] + [vmem] * len(args),
        out_specs=[vmem] * RING,
        scratch_shapes=scratch,
        out_shape=[jax.ShapeDtypeStruct((nb, columns), F32 if s == 0 else BF16) for s in range(RING)],
        compiler_params=params(SUMS_MIB),
        cost_estimate=cost(2 * nb * rows * RING * columns * (1 if flat is None else 2), 4 * nb * rows),
        name="panel_sums",
    )(place, *args)


SUMS_MIB = 12


def coefficients_kernel(factor, a, b, c, d, out):
    total = a[...] + b[...].astype(F32) + c[...].astype(F32) + d[...].astype(F32)
    out[...] = jnp.dot(
        factor[...], total, preferred_element_type=F32, precision=lax.Precision.HIGHEST
    ).astype(BF16)


def coefficients(factor, parts):
    vmem = pl.BlockSpec(memory_space=pltpu.VMEM)
    return pl.pallas_call(
        coefficients_kernel,
        in_specs=[vmem] * 5,
        out_specs=vmem,
        out_shape=jax.ShapeDtypeStruct(parts[0].shape, BF16),
        compiler_params=params(8),
        cost_estimate=cost(12 * factor.size * parts[0].shape[1], 4 * factor.size),
        name="coefficients",
    )(factor, *parts)


def update_kernel(count, width, place, first, second, *refs):
    w0, w1, outs, w = refs[:count], refs[count:2 * count], refs[2 * count:-1], refs[-1]
    rows, nb = first.shape
    take_home(place, w0, width, w.at[:nb])
    take_home(place, w1, width, w.at[nb:])
    halves = len(outs) // count
    height = rows // halves
    for at in range(0, rows, TILE):
        moved = jnp.dot(first[at:at + TILE, :], w[:nb, :], preferred_element_type=F32)
        moved += jnp.dot(second[at:at + TILE, :], w[nb:, :], preferred_element_type=F32)
        for s in range(count):
            out, start = outs[s * halves + at // height], at % height
            out[start:start + TILE, :] = moved[:, s * 128:(s + 1) * 128].astype(BF16)


def update(place, first, second, w0, w1, halves):
    vmem = pl.BlockSpec(memory_space=pltpu.VMEM)
    rows, nb = first.shape
    columns = w0[0].shape[1]
    count = len(w0)
    return pl.pallas_call(
        functools.partial(update_kernel, count, nb // (RING * RING)),
        in_specs=[pl.BlockSpec(memory_space=pltpu.SMEM)] + [vmem] * (2 + 2 * count),
        out_specs=[vmem] * (count * halves),
        out_shape=[jax.ShapeDtypeStruct((rows // halves, columns), BF16)] * (count * halves),
        scratch_shapes=[pltpu.VMEM((2 * nb, count * columns), BF16)],
        compiler_params=params(UPDATE_MIB),
        cost_estimate=cost(4 * nb * rows * count * columns, 4 * nb * rows),
        name="update",
    )(place, first, second, *w0, *w1)


UPDATE_MIB = 10


def subtract_kernel(s, place, z, moved, *refs):
    refs[-1][...] = z[...] - moved[...].astype(F32)


SUB_TILE = 2048


def subtract(place, z, moved, s, half, out):
    tile = SUB_TILE
    rows, columns = moved.shape
    steps = rows // tile
    chunk = z.shape[0] // RING // tile

    def whole(i, place):
        return (lax.rem(place[0] + s, RING) * chunk + half * chunk // 2 + i, 0)

    in_specs = [pl.BlockSpec((tile, columns), whole), pl.BlockSpec((tile, columns), lambda i, place: (i, 0))]
    args = [z, moved]
    if out is not None:
        in_specs.append(pl.BlockSpec(memory_space=pl.ANY))
        args.append(out)
    return pl.pallas_call(
        functools.partial(subtract_kernel, s),
        grid_spec=pltpu.PrefetchScalarGridSpec(
            num_scalar_prefetch=1,
            grid=(steps,),
            in_specs=in_specs,
            out_specs=pl.BlockSpec((tile, columns), whole),
        ),
        out_shape=jax.ShapeDtypeStruct(z.shape, F32),
        input_output_aliases={} if out is None else {3: 0},
        compiler_params=params(8),
        cost_estimate=cost(rows * columns, 10 * rows * columns),
        name="subtract",
    )(place, *args)


def local(z_block, v_panels, t_panels):
    prow, pcol = lax.axis_index("prow"), lax.axis_index("pcol")
    core, y, z = prow % 2, pcol // RING, pcol % RING
    u, w = jnp.where(core == 0, y, z), jnp.where(core == 0, z, y)
    place = jnp.stack([u, w, core]).astype(jnp.int32)
    rows = z_block.shape[0] // RING
    width = v_panels.shape[2]
    tie = lax.optimization_barrier

    def chunk(s):
        return ((u + s) % RING) * rows

    flat = jnp.swapaxes(v_panels, 1, 2).reshape(2 * width, RING * rows)
    mine = [lax.dynamic_slice(flat, (0, chunk(s)), (2 * width, rows)) for s in range(RING)]
    z_in, t_in, mine = tie((z_block, t_panels, mine))
    blocks = [mine[0]] + [send(mine[s], along_u(s)) for s in range(1, RING)]

    def cut(s, start, size):
        return lax.dynamic_slice(z_in, (chunk(s) + start, 0), (size, z_block.shape[1])).astype(BF16)

    own, right, left = cut(0, 0, rows), cut(1, 0, rows), cut(3, 0, rows)
    far = [cut(2, 0, rows // 2), cut(2, rows // 2, rows // 2)]
    factors = jnp.swapaxes(t_in, 1, 2)
    blocks, own, factors = tie((blocks, own, factors))
    block, later = stack(place, blocks)

    half = block.shape[0] // 2
    ahead, behind = send(block, along_w(1)), send(block, along_w(-1))
    right, left = send(right, along_u(1)), send(left, along_u(-1))
    right, left, far = tie((right, left, far))
    far = [send(far[0], along_u(1)), send(far[1], along_u(-1))]
    far_low, far_high = send(ahead[:half], along_w(1)), send(behind[half:], along_w(-1))
    far = [send(far[0], along_u(1)), send(far[1], along_u(-1))]
    first = [block, ahead, far_low, far_high, behind]
    dealt = [own, right, *far, left]
    first, dealt, later, factors = tie((first, dealt, later, factors))

    def reduce(parts, factor, early, late):
        parts = [parts[0]] + [send(parts[s], along_u(-s)) for s in range(1, RING)]
        total = parts[0]
        for part in parts[1:]:
            total = total + part.astype(F32)
        total, early = tie((total, early))
        total = total + send(total, other_core())
        rounded = total.astype(BF16)
        parts = [total] + [send(rounded, along_x(s)) for s in range(1, RING)]
        parts, late = tie((parts, late))
        coeffs = coefficients(factor, parts)
        return [coeffs] + [send(coeffs, along_u(s)) for s in range(1, RING)], early, late

    parts = sums(place, first, dealt)
    parts, later = tie((parts, later))
    ahead, behind = send(later, along_w(1)), send(later, along_w(-1))
    far_low, far_high = send(ahead[:half], along_w(1)), send(behind[half:], along_w(-1))
    second = [later, ahead, far_low, far_high, behind]
    w0, first_flat, _ = reduce(parts, factors[0], transpose(first), ())
    w1, second_flat, _ = reduce(sums(place, second, dealt, first_flat, w0), factors[1], transpose(second), ())

    def moved(shifts, halves):
        return update(place, first_flat, second_flat, [w0[s] for s in shifts], [w1[s] for s in shifts], halves)

    right, left = moved((1, 3), 1)
    right, left = send(right, along_u(-1)), send(left, along_u(1))
    far, own = moved((2, 0), 1)
    far = send(far, along_u(2))
    out = subtract(place, z_block, own, 0, 0, None)
    out = subtract(place, z_block, right, 1, 0, out)
    out = subtract(place, z_block, left, 3, 0, out)
    return subtract(place, z_block, far, 2, 0, out)


def solution(mesh):
    return jax.shard_map(
        local,
        mesh=mesh,
        in_specs=(P("prow", "pcol"), P(None, "prow", "pcol"), P()),
        out_specs=P("prow", "pcol"),
        check_vma=False,
    )
```

```python
import functools

import jax
import jax.numpy as jnp
from jax import lax
from jax.experimental import pallas as pl
from jax.experimental.pallas import tpu as pltpu
from jax.sharding import PartitionSpec as P

RING = 4
BF16, F32 = jnp.bfloat16, jnp.float32
AXES = ("prow", "pcol")


def device(x, core, y, z):
    return (x * 2 + core) * RING * RING + y * RING + z


def permutation(target):
    pairs = []
    for x in range(RING):
        for core in range(2):
            for y in range(RING):
                for z in range(RING):
                    pairs.append((device(x, core, y, z), device(*target(x, core, y, z))))
    return pairs


def along_u(s):
    return permutation(lambda x, c, y, z: (x, c, (y + s) % RING, z) if c == 0 else (x, c, y, (z + s) % RING))


def along_w(s):
    return permutation(lambda x, c, y, z: (x, c, y, (z + s) % RING) if c == 0 else (x, c, (y + s) % RING, z))


def along_x(s):
    return permutation(lambda x, c, y, z: ((x + s) % RING, c, y, z))


def other_core():
    return permutation(lambda x, c, y, z: (x, 1 - c, y, z))


def send(value, pairs):
    return lax.ppermute(value, AXES, pairs)


def params(mib=16):
    return pltpu.CompilerParams(vmem_limit_bytes=mib * 2**20)


def cost(flops, nbytes):
    return pl.CostEstimate(flops=flops, bytes_accessed=nbytes, transcendentals=0)


def home(place, t, k):
    gone = lax.rem(place[1] - t + RING, RING)
    return jnp.where(place[2] == 0, k * RING + gone, gone * RING + k)


def block_rows(at, width):
    return pl.ds(pl.multiple_of(at * width, width), width)


def stack_kernel(place, *refs):
    blocks, outs = refs[:RING], refs[RING:]
    width = blocks[0].shape[0] // 2
    for s in range(RING):
        rows = block_rows(lax.rem(place[0] - s + RING, RING), width)
        for panel in range(2):
            outs[panel][rows, :] = blocks[s][panel * width:(panel + 1) * width, :]


def stack(place, blocks):
    height, rows = blocks[0].shape
    tile = rows // 4
    out = jax.ShapeDtypeStruct((RING * height // 2, rows), BF16)
    return pl.pallas_call(
        stack_kernel,
        grid_spec=pltpu.PrefetchScalarGridSpec(
            num_scalar_prefetch=1,
            grid=(rows // tile,),
            in_specs=[pl.BlockSpec((height, tile), lambda i, place: (0, i))] * RING,
            out_specs=[pl.BlockSpec((RING * height // 2, tile), lambda i, place: (0, i))] * 2,
        ),
        out_shape=[out, out],
        compiler_params=params(8),
        cost_estimate=cost(0, 4 * RING * height * rows),
        name="stack_reflectors",
    )(place, *blocks)


def transpose_kernel(*refs):
    out = refs[-1]
    at = 0
    for r in refs[:-1]:
        out[:, at:at + r.shape[0]] = r[...].T
        at += r.shape[0]


def transpose(blocks):
    rows = blocks[0].shape[1]
    nb = sum(b.shape[0] for b in blocks)
    tile = 1024
    return pl.pallas_call(
        transpose_kernel,
        grid=(rows // tile,),
        in_specs=[pl.BlockSpec((b.shape[0], tile), lambda i: (0, i)) for b in blocks],
        out_specs=pl.BlockSpec((tile, nb), lambda i: (i, 0)),
        out_shape=jax.ShapeDtypeStruct((rows, nb), BF16),
        compiler_params=params(8),
        cost_estimate=cost(0, 4 * nb * rows),
        name="transpose_reflectors",
    )(*blocks)


def put_home(place, total, outs, width):
    for s in range(RING):
        for t in range(RING):
            for k in range(RING):
                at = t * RING + k
                outs[s][block_rows(home(place, t, k), width), :] = total[
                    at * width:(at + 1) * width, s * 128:(s + 1) * 128
                ].astype(outs[s].dtype)


def take_home(place, sources, width, out):
    for s, source in enumerate(sources):
        for t in range(RING):
            for k in range(RING):
                at = t * RING + k
                out[at * width:(at + 1) * width, s * 128:(s + 1) * 128] = source[block_rows(home(place, t, k), width), :]


TILE = 1024
NEAR_FIRST = (0, 1, 3, 2)


def tiles_of(z, tile):
    own, right, far_low, far_high, left = z
    steps = own.shape[0] // tile
    for i in range(steps):
        far = far_low if i < steps // 2 else far_high
        at = (i % (steps // 2)) * tile
        rows = slice(i * tile, (i + 1) * tile)
        yield rows, [own[rows, :], right[rows, :], far[at:at + tile, :], left[rows, :]]


def first_sums_kernel(count, width, place, *refs):
    v, z = refs[:count], refs[count:count + RING + 1]
    outs, total = refs[count + RING + 1:-1], refs[-1]
    for rows, parts in tiles_of(z, TILE):
        left = jnp.concatenate([r[:, rows] for r in v], axis=0)
        part = jnp.dot(left, jnp.concatenate(parts, axis=1), preferred_element_type=F32)
        if rows.start:
            total[...] += part
        else:
            total[...] = part
    put_home(place, total, outs, width)


def second_sums_kernel(count, width, place, *refs):
    v, z, flat = refs[:count], refs[count:count + RING + 1], refs[count + RING + 1]
    coeffs = refs[count + RING + 2:count + 2 * RING + 2]
    outs, total, w = refs[count + 2 * RING + 2:-2], refs[-2], refs[-1]
    take_home(place, [coeffs[NEAR_FIRST.index(s)] for s in range(RING)], width, w)
    for rows, parts in tiles_of(z, TILE):
        left = jnp.concatenate([r[:, rows] for r in v], axis=0)
        old = jnp.concatenate(parts, axis=1).astype(F32)
        right = (old - jnp.dot(flat[rows, :], w[...], preferred_element_type=F32)).astype(BF16)
        part = jnp.dot(left, right, preferred_element_type=F32)
        if rows.start:
            total[...] += part
        else:
            total[...] = part
    put_home(place, total, outs, width)


def sums(place, v, z, flat=None, coeffs=()):
    vmem = pl.BlockSpec(memory_space=pltpu.VMEM)
    rows = v[0].shape[1]
    columns = z[0].shape[1]
    nb = sum(b.shape[0] for b in v)
    width = nb // (RING * RING)
    args = list(v) + list(z)
    scratch = [pltpu.VMEM((nb, RING * columns), F32)]
    if flat is not None:
        args += [flat, *(coeffs[s] for s in NEAR_FIRST)]
        scratch += [pltpu.VMEM((nb, RING * columns), BF16)]
    return pl.pallas_call(
        functools.partial(first_sums_kernel if flat is None else second_sums_kernel, len(v), width),
        in_specs=[pl.BlockSpec(memory_space=pltpu.SMEM)] + [vmem] * len(args),
        out_specs=[vmem] * RING,
        scratch_shapes=scratch,
        out_shape=[jax.ShapeDtypeStruct((nb, columns), F32 if s == 0 else BF16) for s in range(RING)],
        compiler_params=params(SUMS_MIB),
        cost_estimate=cost(2 * nb * rows * RING * columns * (1 if flat is None else 2), 4 * nb * rows),
        name="panel_sums",
    )(place, *args)


SUMS_MIB = 12


def coefficients_kernel(factor, a, b, c, d, out):
    total = a[...] + b[...].astype(F32) + c[...].astype(F32) + d[...].astype(F32)
    out[...] = jnp.dot(
        factor[...], total, preferred_element_type=F32, precision=lax.Precision.HIGHEST
    ).astype(BF16)


def coefficients(factor, parts):
    vmem = pl.BlockSpec(memory_space=pltpu.VMEM)
    return pl.pallas_call(
        coefficients_kernel,
        in_specs=[vmem] * 5,
        out_specs=vmem,
        out_shape=jax.ShapeDtypeStruct(parts[0].shape, BF16),
        compiler_params=params(8),
        cost_estimate=cost(12 * factor.size * parts[0].shape[1], 4 * factor.size),
        name="coefficients",
    )(factor, *parts)


def update_kernel(count, width, place, first, second, *refs):
    w0, w1, outs, w = refs[:count], refs[count:2 * count], refs[2 * count:-1], refs[-1]
    rows, nb = first.shape
    take_home(place, w0, width, w.at[:nb])
    take_home(place, w1, width, w.at[nb:])
    halves = len(outs) // count
    height = rows // halves
    for at in range(0, rows, TILE):
        moved = jnp.dot(first[at:at + TILE, :], w[:nb, :], preferred_element_type=F32)
        moved += jnp.dot(second[at:at + TILE, :], w[nb:, :], preferred_element_type=F32)
        for s in range(count):
            out, start = outs[s * halves + at // height], at % height
            out[start:start + TILE, :] = moved[:, s * 128:(s + 1) * 128].astype(BF16)


def update(place, first, second, w0, w1, halves):
    vmem = pl.BlockSpec(memory_space=pltpu.VMEM)
    rows, nb = first.shape
    columns = w0[0].shape[1]
    count = len(w0)
    return pl.pallas_call(
        functools.partial(update_kernel, count, nb // (RING * RING)),
        in_specs=[pl.BlockSpec(memory_space=pltpu.SMEM)] + [vmem] * (2 + 2 * count),
        out_specs=[vmem] * (count * halves),
        out_shape=[jax.ShapeDtypeStruct((rows // halves, columns), BF16)] * (count * halves),
        scratch_shapes=[pltpu.VMEM((2 * nb, count * columns), BF16)],
        compiler_params=params(UPDATE_MIB),
        cost_estimate=cost(4 * nb * rows * count * columns, 4 * nb * rows),
        name="update",
    )(place, first, second, *w0, *w1)


UPDATE_MIB = 10


def subtract_kernel(s, place, z, moved, *refs):
    refs[-1][...] = z[...] - moved[...].astype(F32)


SUB_TILE = 2048


def subtract(place, z, moved, s, half, out):
    tile = SUB_TILE
    rows, columns = moved.shape
    steps = rows // tile
    chunk = z.shape[0] // RING // tile

    def whole(i, place):
        return (lax.rem(place[0] + s, RING) * chunk + half * chunk // 2 + i, 0)

    in_specs = [pl.BlockSpec((tile, columns), whole), pl.BlockSpec((tile, columns), lambda i, place: (i, 0))]
    args = [z, moved]
    if out is not None:
        in_specs.append(pl.BlockSpec(memory_space=pl.ANY))
        args.append(out)
    return pl.pallas_call(
        functools.partial(subtract_kernel, s),
        grid_spec=pltpu.PrefetchScalarGridSpec(
            num_scalar_prefetch=1,
            grid=(steps,),
            in_specs=in_specs,
            out_specs=pl.BlockSpec((tile, columns), whole),
        ),
        out_shape=jax.ShapeDtypeStruct(z.shape, F32),
        input_output_aliases={} if out is None else {3: 0},
        compiler_params=params(8),
        cost_estimate=cost(rows * columns, 10 * rows * columns),
        name="subtract",
    )(place, *args)


def local(z_block, v_panels, t_panels):
    prow, pcol = lax.axis_index("prow"), lax.axis_index("pcol")
    core, y, z = prow % 2, pcol // RING, pcol % RING
    u, w = jnp.where(core == 0, y, z), jnp.where(core == 0, z, y)
    place = jnp.stack([u, w, core]).astype(jnp.int32)
    rows = z_block.shape[0] // RING
    width = v_panels.shape[2]
    tie = lax.optimization_barrier

    def chunk(s):
        return ((u + s) % RING) * rows

    flat = jnp.swapaxes(v_panels, 1, 2).reshape(2 * width, RING * rows)
    mine = [lax.dynamic_slice(flat, (0, chunk(s)), (2 * width, rows)) for s in range(RING)]
    z_in, t_in, mine = tie((z_block, t_panels, mine))
    blocks = [mine[0]] + [send(mine[s], along_u(s)) for s in range(1, RING)]

    def cut(s, start, size):
        return lax.dynamic_slice(z_in, (chunk(s) + start, 0), (size, z_block.shape[1])).astype(BF16)

    own, right, left = cut(0, 0, rows), cut(1, 0, rows), cut(3, 0, rows)
    far = [cut(2, 0, rows // 2), cut(2, rows // 2, rows // 2)]
    factors = jnp.swapaxes(t_in, 1, 2)
    blocks, own, factors = tie((blocks, own, factors))
    block, later = stack(place, blocks)

    half = block.shape[0] // 2
    ahead, behind = send(block, along_w(1)), send(block, along_w(-1))
    right, left = send(right, along_u(1)), send(left, along_u(-1))
    right, left, far = tie((right, left, far))
    far = [send(far[0], along_u(1)), send(far[1], along_u(-1))]
    far_low, far_high = send(ahead[:half], along_w(1)), send(behind[half:], along_w(-1))
    far = [send(far[0], along_u(1)), send(far[1], along_u(-1))]
    first = [block, ahead, far_low, far_high, behind]
    dealt = [own, right, *far, left]
    first, dealt, later, factors = tie((first, dealt, later, factors))

    def reduce(parts, factor, early, late):
        moved = {s: send(parts[s], along_u(-s)) for s in (2, 1, 3)}
        parts = [parts[0]] + [moved[s] for s in (2, 1, 3)]
        total = parts[0]
        for part in parts[1:]:
            total = total + part.astype(F32)
        total, early = tie((total, early))
        total = total + send(total, other_core())
        rounded = total.astype(BF16)
        parts = [total] + [send(rounded, along_x(s)) for s in (1, 3, 2)]
        parts, late = tie((parts, late))
        coeffs = coefficients(factor, parts)
        moved = {s: send(coeffs, along_u(s)) for s in (1, 3, 2)}
        return [coeffs, moved[1], moved[2], moved[3]], early, late

    parts = sums(place, first, dealt)
    parts, later = tie((parts, later))
    ahead, behind = send(later, along_w(1)), send(later, along_w(-1))
    far_low, far_high = send(ahead[:half], along_w(1)), send(behind[half:], along_w(-1))
    second = [later, ahead, far_low, far_high, behind]
    w0, first_flat, _ = reduce(parts, factors[0], transpose(first), ())
    w1, second_flat, _ = reduce(sums(place, second, dealt, first_flat, w0), factors[1], transpose(second), ())

    def moved(shifts, halves):
        return update(place, first_flat, second_flat, [w0[s] for s in shifts], [w1[s] for s in shifts], halves)

    right, left = moved((1, 3), 1)
    right, left = send(right, along_u(-1)), send(left, along_u(1))
    far, own = moved((2, 0), 1)
    far = send(far, along_u(2))
    out = subtract(place, z_block, own, 0, 0, None)
    out = subtract(place, z_block, right, 1, 0, out)
    out = subtract(place, z_block, left, 3, 0, out)
    return subtract(place, z_block, far, 2, 0, out)


def solution(mesh):
    return jax.shard_map(
        local,
        mesh=mesh,
        in_specs=(P("prow", "pcol"), P(None, "prow", "pcol"), P()),
        out_specs=P("prow", "pcol"),
        check_vma=False,
    )
```

```python
import functools

import jax
import jax.numpy as jnp
from jax import lax
from jax.experimental import pallas as pl
from jax.experimental.pallas import tpu as pltpu
from jax.sharding import PartitionSpec as P

RING = 4
BF16, F32 = jnp.bfloat16, jnp.float32
AXES = ("prow", "pcol")


def device(x, core, y, z):
    return (x * 2 + core) * RING * RING + y * RING + z


def permutation(target):
    pairs = []
    for x in range(RING):
        for core in range(2):
            for y in range(RING):
                for z in range(RING):
                    pairs.append((device(x, core, y, z), device(*target(x, core, y, z))))
    return pairs


def along_u(s):
    return permutation(lambda x, c, y, z: (x, c, (y + s) % RING, z) if c == 0 else (x, c, y, (z + s) % RING))


def along_w(s):
    return permutation(lambda x, c, y, z: (x, c, y, (z + s) % RING) if c == 0 else (x, c, (y + s) % RING, z))


def along_x(s):
    return permutation(lambda x, c, y, z: ((x + s) % RING, c, y, z))


def other_core():
    return permutation(lambda x, c, y, z: (x, 1 - c, y, z))


def send(value, pairs):
    return lax.ppermute(value, AXES, pairs)


def params(mib=16):
    return pltpu.CompilerParams(vmem_limit_bytes=mib * 2**20)


def cost(flops, nbytes):
    return pl.CostEstimate(flops=flops, bytes_accessed=nbytes, transcendentals=0)


def home(place, t, k):
    gone = lax.rem(place[1] - t + RING, RING)
    return jnp.where(place[2] == 0, k * RING + gone, gone * RING + k)


def block_rows(at, width):
    return pl.ds(pl.multiple_of(at * width, width), width)


def stack_kernel(place, *refs):
    blocks, outs = refs[:RING], refs[RING:]
    width = blocks[0].shape[0] // 2
    for s in range(RING):
        rows = block_rows(lax.rem(place[0] - s + RING, RING), width)
        for panel in range(2):
            outs[panel][rows, :] = blocks[s][panel * width:(panel + 1) * width, :]


def stack(place, blocks):
    height, rows = blocks[0].shape
    tile = rows // 4
    out = jax.ShapeDtypeStruct((RING * height // 2, rows), BF16)
    return pl.pallas_call(
        stack_kernel,
        grid_spec=pltpu.PrefetchScalarGridSpec(
            num_scalar_prefetch=1,
            grid=(rows // tile,),
            in_specs=[pl.BlockSpec((height, tile), lambda i, place: (0, i))] * RING,
            out_specs=[pl.BlockSpec((RING * height // 2, tile), lambda i, place: (0, i))] * 2,
        ),
        out_shape=[out, out],
        compiler_params=params(8),
        cost_estimate=cost(0, 4 * RING * height * rows),
        name="stack_reflectors",
    )(place, *blocks)


def transpose_kernel(*refs):
    out = refs[-1]
    at = 0
    for r in refs[:-1]:
        out[:, at:at + r.shape[0]] = r[...].T
        at += r.shape[0]


def transpose(blocks):
    rows = blocks[0].shape[1]
    nb = sum(b.shape[0] for b in blocks)
    tile = 1024
    return pl.pallas_call(
        transpose_kernel,
        grid=(rows // tile,),
        in_specs=[pl.BlockSpec((b.shape[0], tile), lambda i: (0, i)) for b in blocks],
        out_specs=pl.BlockSpec((tile, nb), lambda i: (i, 0)),
        out_shape=jax.ShapeDtypeStruct((rows, nb), BF16),
        compiler_params=params(8),
        cost_estimate=cost(0, 4 * nb * rows),
        name="transpose_reflectors",
    )(*blocks)


def put_home(place, total, outs, width):
    for s in range(RING):
        for t in range(RING):
            for k in range(RING):
                at = t * RING + k
                outs[s][block_rows(home(place, t, k), width), :] = total[
                    at * width:(at + 1) * width, s * 128:(s + 1) * 128
                ].astype(outs[s].dtype)


def take_home(place, sources, width, out):
    for s, source in enumerate(sources):
        for t in range(RING):
            for k in range(RING):
                at = t * RING + k
                out[at * width:(at + 1) * width, s * 128:(s + 1) * 128] = source[block_rows(home(place, t, k), width), :]


TILE = 1024
NEAR_FIRST = (0, 1, 3, 2)


def tiles_of(z, tile):
    own, right, far_low, far_high, left = z
    steps = own.shape[0] // tile
    for i in range(steps):
        far = far_low if i < steps // 2 else far_high
        at = (i % (steps // 2)) * tile
        rows = slice(i * tile, (i + 1) * tile)
        yield rows, [own[rows, :], right[rows, :], far[at:at + tile, :], left[rows, :]]


def first_sums_kernel(count, width, place, *refs):
    v, z = refs[:count], refs[count:count + RING + 1]
    outs, total = refs[count + RING + 1:-1], refs[-1]
    for rows, parts in tiles_of(z, TILE):
        left = jnp.concatenate([r[:, rows] for r in v], axis=0)
        part = jnp.dot(left, jnp.concatenate(parts, axis=1), preferred_element_type=F32)
        if rows.start:
            total[...] += part
        else:
            total[...] = part
    put_home(place, total, outs, width)


def second_sums_kernel(count, width, place, *refs):
    v, z, flat = refs[:count], refs[count:count + RING + 1], refs[count + RING + 1]
    coeffs = refs[count + RING + 2:count + 2 * RING + 2]
    outs, total, w = refs[count + 2 * RING + 2:-2], refs[-2], refs[-1]
    take_home(place, [coeffs[NEAR_FIRST.index(s)] for s in range(RING)], width, w)
    for rows, parts in tiles_of(z, TILE):
        left = jnp.concatenate([r[:, rows] for r in v], axis=0)
        old = jnp.concatenate(parts, axis=1).astype(F32)
        right = (old - jnp.dot(flat[rows, :], w[...], preferred_element_type=F32)).astype(BF16)
        part = jnp.dot(left, right, preferred_element_type=F32)
        if rows.start:
            total[...] += part
        else:
            total[...] = part
    put_home(place, total, outs, width)


def sums(place, v, z, flat=None, coeffs=()):
    vmem = pl.BlockSpec(memory_space=pltpu.VMEM)
    rows = v[0].shape[1]
    columns = z[0].shape[1]
    nb = sum(b.shape[0] for b in v)
    width = nb // (RING * RING)
    args = list(v) + list(z)
    scratch = [pltpu.VMEM((nb, RING * columns), F32)]
    if flat is not None:
        args += [flat, *(coeffs[s] for s in NEAR_FIRST)]
        scratch += [pltpu.VMEM((nb, RING * columns), BF16)]
    return pl.pallas_call(
        functools.partial(first_sums_kernel if flat is None else second_sums_kernel, len(v), width),
        in_specs=[pl.BlockSpec(memory_space=pltpu.SMEM)] + [vmem] * len(args),
        out_specs=[vmem] * RING,
        scratch_shapes=scratch,
        out_shape=[jax.ShapeDtypeStruct((nb, columns), F32 if s == 0 else BF16) for s in range(RING)],
        compiler_params=params(SUMS_MIB),
        cost_estimate=cost(2 * nb * rows * RING * columns * (1 if flat is None else 2), 4 * nb * rows),
        name="panel_sums",
    )(place, *args)


SUMS_MIB = 12


def coefficients_kernel(factor, a, b, c, d, out):
    total = a[...] + b[...].astype(F32) + c[...].astype(F32) + d[...].astype(F32)
    out[...] = jnp.dot(
        factor[...], total, preferred_element_type=F32, precision=lax.Precision.HIGHEST
    ).astype(BF16)


def coefficients(factor, parts):
    vmem = pl.BlockSpec(memory_space=pltpu.VMEM)
    return pl.pallas_call(
        coefficients_kernel,
        in_specs=[vmem] * 5,
        out_specs=vmem,
        out_shape=jax.ShapeDtypeStruct(parts[0].shape, BF16),
        compiler_params=params(8),
        cost_estimate=cost(12 * factor.size * parts[0].shape[1], 4 * factor.size),
        name="coefficients",
    )(factor, *parts)


def update_kernel(count, width, place, first, second, *refs):
    w0, w1, outs, w = refs[:count], refs[count:2 * count], refs[2 * count:-1], refs[-1]
    rows, nb = first.shape
    take_home(place, w0, width, w.at[:nb])
    take_home(place, w1, width, w.at[nb:])
    halves = len(outs) // count
    height = rows // halves
    for at in range(0, rows, TILE):
        moved = jnp.dot(first[at:at + TILE, :], w[:nb, :], preferred_element_type=F32)
        moved += jnp.dot(second[at:at + TILE, :], w[nb:, :], preferred_element_type=F32)
        for s in range(count):
            out, start = outs[s * halves + at // height], at % height
            out[start:start + TILE, :] = moved[:, s * 128:(s + 1) * 128].astype(BF16)


def update(place, first, second, w0, w1, halves):
    vmem = pl.BlockSpec(memory_space=pltpu.VMEM)
    rows, nb = first.shape
    columns = w0[0].shape[1]
    count = len(w0)
    return pl.pallas_call(
        functools.partial(update_kernel, count, nb // (RING * RING)),
        in_specs=[pl.BlockSpec(memory_space=pltpu.SMEM)] + [vmem] * (2 + 2 * count),
        out_specs=[vmem] * (count * halves),
        out_shape=[jax.ShapeDtypeStruct((rows // halves, columns), BF16)] * (count * halves),
        scratch_shapes=[pltpu.VMEM((2 * nb, count * columns), BF16)],
        compiler_params=params(UPDATE_MIB),
        cost_estimate=cost(4 * nb * rows * count * columns, 4 * nb * rows),
        name="update",
    )(place, first, second, *w0, *w1)


UPDATE_MIB = 10


def subtract_kernel(s, place, z, moved, *refs):
    refs[-1][...] = z[...] - moved[...].astype(F32)


SUB_TILE = 2048


def subtract(place, z, moved, s, half, out):
    tile = SUB_TILE
    rows, columns = moved.shape
    steps = rows // tile
    chunk = z.shape[0] // RING // tile

    def whole(i, place):
        return (lax.rem(place[0] + s, RING) * chunk + half * chunk // 2 + i, 0)

    in_specs = [pl.BlockSpec((tile, columns), whole), pl.BlockSpec((tile, columns), lambda i, place: (i, 0))]
    args = [z, moved]
    if out is not None:
        in_specs.append(pl.BlockSpec(memory_space=pl.ANY))
        args.append(out)
    return pl.pallas_call(
        functools.partial(subtract_kernel, s),
        grid_spec=pltpu.PrefetchScalarGridSpec(
            num_scalar_prefetch=1,
            grid=(steps,),
            in_specs=in_specs,
            out_specs=pl.BlockSpec((tile, columns), whole),
        ),
        out_shape=jax.ShapeDtypeStruct(z.shape, F32),
        input_output_aliases={} if out is None else {3: 0},
        compiler_params=params(8),
        cost_estimate=cost(rows * columns, 10 * rows * columns),
        name="subtract",
    )(place, *args)


def local(z_block, v_panels, t_panels):
    prow, pcol = lax.axis_index("prow"), lax.axis_index("pcol")
    core, y, z = prow % 2, pcol // RING, pcol % RING
    u, w = jnp.where(core == 0, y, z), jnp.where(core == 0, z, y)
    place = jnp.stack([u, w, core]).astype(jnp.int32)
    rows = z_block.shape[0] // RING
    width = v_panels.shape[2]
    tie = lax.optimization_barrier

    def chunk(s):
        return ((u + s) % RING) * rows

    flat = jnp.swapaxes(v_panels, 1, 2).reshape(2 * width, RING * rows)
    mine = [lax.dynamic_slice(flat, (0, chunk(s)), (2 * width, rows)) for s in range(RING)]
    z_in, t_in, mine = tie((z_block, t_panels, mine))
    blocks = [mine[0]] + [send(mine[s], along_u(s)) for s in range(1, RING)]

    def cut(s, start, size):
        return lax.dynamic_slice(z_in, (chunk(s) + start, 0), (size, z_block.shape[1])).astype(BF16)

    own, right, left = cut(0, 0, rows), cut(1, 0, rows), cut(3, 0, rows)
    far = [cut(2, 0, rows // 2), cut(2, rows // 2, rows // 2)]
    factors = jnp.swapaxes(t_in, 1, 2)
    blocks, own, factors = tie((blocks, own, factors))
    block, later = stack(place, blocks)

    half = block.shape[0] // 2
    ahead, behind = send(block, along_w(1)), send(block, along_w(-1))
    right, left = send(right, along_u(1)), send(left, along_u(-1))
    right, left, far = tie((right, left, far))
    far = [send(far[0], along_u(1)), send(far[1], along_u(-1))]
    far_low, far_high = send(ahead[:half], along_w(1)), send(behind[half:], along_w(-1))
    far = [send(far[0], along_u(1)), send(far[1], along_u(-1))]
    first = [block, ahead, far_low, far_high, behind]
    dealt = [own, right, *far, left]
    first, dealt, later, factors = tie((first, dealt, later, factors))

    def reduce(parts, factor, early, late):
        moved = {s: send(parts[s], along_u(-s)) for s in (2, 1, 3)}
        parts = [parts[0]] + [moved[s] for s in (2, 1, 3)]
        total = parts[0]
        for part in parts[1:]:
            total = total + part.astype(F32)
        total, early = tie((total, early))
        total = total + send(total, other_core())
        rounded = total.astype(BF16)
        parts = [total] + [send(rounded, along_x(s)) for s in (1, 3, 2)]
        parts, late = tie((parts, late))
        coeffs = coefficients(factor, parts)
        moved = {s: send(coeffs, along_u(s)) for s in (1, 3, 2)}
        return [coeffs, moved[1], moved[2], moved[3]], early, late

    parts = sums(place, first, dealt)
    parts, later = tie((parts, later))
    ahead, behind = send(later, along_w(1)), send(later, along_w(-1))
    far_low, far_high = send(ahead[:half], along_w(1)), send(behind[half:], along_w(-1))
    second = [later, ahead, far_low, far_high, behind]
    w0, first_flat, _ = reduce(parts, factors[0], transpose(first), ())
    w1, second_flat, _ = reduce(sums(place, second, dealt, first_flat, w0), factors[1], transpose(second), ())

    def moved(shifts, halves):
        return update(place, first_flat, second_flat, [w0[s] for s in shifts], [w1[s] for s in shifts], halves)

    own, = moved((0,), 1)
    right, left = moved((1, 3), 1)
    right, left = send(right, along_u(-1)), send(left, along_u(1))
    far, = moved((2,), 1)
    far = send(far, along_u(2))
    out = subtract(place, z_block, own, 0, 0, None)
    out = subtract(place, z_block, right, 1, 0, out)
    out = subtract(place, z_block, left, 3, 0, out)
    return subtract(place, z_block, far, 2, 0, out)


def solution(mesh):
    return jax.shard_map(
        local,
        mesh=mesh,
        in_specs=(P("prow", "pcol"), P(None, "prow", "pcol"), P()),
        out_specs=P("prow", "pcol"),
        check_vma=False,
    )
```
